32 devices in a mesh: lat: 4 (over y, core), grp: 8 (over z, x).
Axes of the slice: x: 2, y: 2, z: 4, core: 2. Of those that a mesh axis runs over, the one named last changes fastest.
Arguments:
- inputs: bfloat16 [256, 1024, 1024], P(None, ('lat', 'grp')), may hold values from -6 to 6
- w_in: bfloat16 [256, 512], replicated, may hold values from -0.375 to 0.375
- bias_in: float32 [512], replicated, may hold values from -3 to 3
- w_out: bfloat16 [512, 256], replicated, may hold values from -0.25 to 0.25
- advected: bfloat16 [256, 1024, 1024], P('grp', 'lat'), may hold values from -6 to 6
- cotangent: bfloat16 [256, 1024, 1024], P('grp', 'lat'), may hold values from -6 to 6
- offsets: int32 [2, 64, 4], P(None, 'lat'), may hold values from 0 to 3
- stencil_row: int32 [64, 4], P('lat'), may hold values from 0 to 4
- stencil_col: int32 [64, 4], P('lat'), may hold values from 0 to 124
- fracs: float32 [2, 64, 4], P(None, 'lat'), may hold values from 0 to 1
Outputs:
- grad_inputs: bfloat16 [256, 1024, 1024], P(None, ('lat', 'grp'))
- grad_w_in: float32 [256, 512], P(None, ('lat', 'grp'))
- grad_bias: float32 [512], P(('lat', 'grp'))
- grad_w_out: float32 [512, 256], P(('lat', 'grp'))
- grad_frac: float32 [2, 64, 4], P(None, 'lat')
The draws below stay inside these ranges and needn't reach their ends.
All inputs are finite; a program needn't handle non-finite values.
Results may differ from the reference program's by a relative error of at most 0.0068.
Values may be sent and summed in bfloat16 or wider, within the bound.
A program may use at most 256 MiB of HBM per device.

```python
import jax
import jax.numpy as jnp
from jax import lax

C = 256
HID = 512
WCOL = 1024
BH = 16
BW = 256
NROWS = 1024
RBLK = 64
CBLK = 4


def with_ends(values, own_key, low, largest):
    longest = values.shape.index(max(values.shape))
    spots = []
    for shift in (0, 1):
        where = [jax.random.randint(jax.random.fold_in(own_key, axis), (), 0, length) for axis, length in enumerate(values.shape)]
        where[longest] = (where[longest] + shift) % values.shape[longest]
        spots.append(tuple(where))
    return values.at[spots[0]].set(low).at[spots[1]].set(largest)


def levels(stream_key, dims, cuts, smallest, high):
    level, own = 1.0, jax.random.fold_in(stream_key, 6)
    for dim, parts in cuts:
        steps = jnp.exp(jax.random.uniform(jax.random.fold_in(own, dim), (parts,), jnp.float32, smallest / len(cuts), high / len(cuts)))
        level = level * jnp.repeat(steps, dims[dim] // parts).reshape([-1 if axis == dim else 1 for axis in range(len(dims))])
    return level


def noise(rng, extent, scale, bound, cuts=(), held_as=jnp.bfloat16):
    array = jax.random.normal(rng, extent, jnp.float32) * scale
    if len(cuts) > 0:
        array = levels(rng, extent, cuts, -0.22, 0.18) * array
    return jnp.clip(array, min=-bound, max=bound).astype(held_as)


def setup_inputs(seed: int = 0) -> dict:
    seeds = jax.random.split(jax.random.key(seed), 11)
    return {
        "inputs": noise(seeds[0], (C, NROWS, WCOL), 1.0, 6.0, ((1, 32),)),
        "w_in": noise(seeds[1], (C, HID), C ** -0.5, 0.375),
        "bias_in": noise(seeds[2], (HID,), 0.5, 3.0, (), jnp.float32),
        "w_out": noise(seeds[3], (HID, C), HID ** -0.5, 0.25),
        "advected": noise(seeds[4], (C, NROWS, WCOL), 1.0, 6.0, ((0, 8), (1, 4))),
        "cotangent": noise(seeds[5], (C, NROWS, WCOL), 1.0, 6.0, ((0, 8), (1, 4))),
        "offsets": with_ends(jax.random.randint(seeds[6], (2, RBLK, CBLK), 0, 4), jax.random.fold_in(seeds[6], 1), 0, 3).astype(jnp.int32),
        "stencil_row": with_ends(jax.random.randint(seeds[7], (RBLK, CBLK), 0, BH // 2 - 3), jax.random.fold_in(seeds[7], 1), 0, (BH // 2 - 3) - 1).astype(jnp.int32),
        "stencil_col": with_ends(jax.random.randint(seeds[8], (RBLK, CBLK), 0, BW // 2 - 3), jax.random.fold_in(seeds[8], 1), 0, (BW // 2 - 3) - 1).astype(jnp.int32),
        "fracs": jnp.clip(1.0 * jax.random.uniform(seeds[9], (2, RBLK, CBLK), jnp.float32) ** levels(seeds[9], (2, RBLK, CBLK), ((1, 4),), -0.2, 0.2), 0.0, 1.0),
    }


def catmull(frac):
    square = frac * frac
    cube = square * frac
    weights = (0.5 * (-cube + 2.0 * square - frac), 0.5 * (3.0 * cube - 5.0 * square + 2.0), 0.5 * (-3.0 * cube + 4.0 * square + frac), 0.5 * (cube - square))
    slopes = (0.5 * (-3.0 * square + 4.0 * frac - 1.0), 0.5 * (9.0 * square - 10.0 * frac), 0.5 * (-9.0 * square + 8.0 * frac + 1.0), 0.5 * (3.0 * square - 2.0 * frac))
    return (weights, slopes)

def band_matrix(position, frac, inner):
    offset_grid = jnp.arange(3 * inner, dtype=jnp.int32)[None, None, :] - jnp.arange(inner, dtype=jnp.int32)[None, :, None] - position[:, None, None]
    weights, slopes = catmull(frac)
    value = jnp.zeros(offset_grid.shape, frac.dtype)
    slope = jnp.zeros(offset_grid.shape, frac.dtype)
    for tap in range(4):
        value = value + jnp.where(offset_grid == tap, weights[tap][:, None, None], 0.0)
        slope = slope + jnp.where(offset_grid == tap, slopes[tap][:, None, None], 0.0)
    return (value.astype(jnp.bfloat16), slope.astype(jnp.bfloat16))

def row_pass(drow, window, row_pos, row_frac, col_pos, col_frac):
    channels = drow.shape[0]
    blocks = drow.shape[2] // BW
    ry_value, ry_slope = band_matrix(row_pos, row_frac, BH)
    rx_value, rx_slope = band_matrix(col_pos, col_frac, BW)
    rx_both = jnp.concatenate([rx_value, rx_slope], axis=2).astype(jnp.float32)
    pieces = drow.reshape(channels, BH, blocks, BW).astype(jnp.float32)
    product = jnp.einsum('chbw,bwv->bchv', pieces, rx_both)
    z_value = product[..., :3 * BW]
    z_slope = product[..., 3 * BW:]
    z_round = z_value.astype(jnp.bfloat16).astype(jnp.float32)
    spread = jnp.einsum('bho,bchv->bcov', ry_value.astype(jnp.float32), z_round)
    windows = jnp.stack([window[:, :, column * BW:column * BW + 3 * BW] for column in range(blocks)])
    ry_both = jnp.concatenate([ry_value, ry_slope], axis=1).astype(jnp.float32)
    lifted = jnp.einsum('bjo,bcov->bcjv', ry_both, windows.astype(jnp.float32))
    grad_row = lax.optimization_barrier(jnp.sum(lifted[:, :, BH:] * z_value, axis=(1, 2, 3)))
    grad_col = lax.optimization_barrier(jnp.sum(lifted[:, :, :BH] * z_slope, axis=(1, 2, 3)))
    split = spread.reshape(blocks, channels, 3, BH, 3, BW)
    summed = jnp.roll(split[:, :, :, :, 0, :], -1, axis=0)
    summed = summed + split[:, :, :, :, 1, :]
    summed = summed + jnp.roll(split[:, :, :, :, 2, :], 1, axis=0)
    contrib = summed.transpose(2, 1, 3, 0, 4).reshape(3, channels, BH, blocks * BW)
    return (contrib, jnp.stack([grad_row, grad_col]))

def reference(inputs, w_in, bias_in, w_out, advected, cotangent, offsets, stencil_row, stencil_col, fracs):
    padded = jnp.pad(advected, ((0, 0), (BH, BH), (0, 0)))
    widened = jnp.concatenate([padded[:, :, WCOL - BW:], padded, padded[:, :, :BW]], axis=2)
    row_pos = BH // 2 * offsets[0] + stencil_row
    col_pos = BW // 2 * offsets[1] + stencil_col

    def one_row(index):
        drow = lax.dynamic_slice_in_dim(cotangent, index * BH, BH, 1)
        window = lax.dynamic_slice_in_dim(widened, index * BH, 3 * BH, 1)
        return row_pass(drow, window, row_pos[index], fracs[0][index], col_pos[index], fracs[1][index])
    contribs, frac_terms = lax.map(one_row, jnp.arange(RBLK, dtype=jnp.int32))
    extended = jnp.zeros((RBLK + 2, C, BH, WCOL), contribs.dtype)
    for shift in range(3):
        extended = extended + jnp.pad(contribs[:, shift], ((shift, 2 - shift), (0, 0), (0, 0), (0, 0)))
    dy = extended[1:RBLK + 1].transpose(1, 0, 2, 3).reshape(C, NROWS, WCOL).astype(jnp.bfloat16)
    grad_frac = jnp.transpose(frac_terms, (1, 0, 2)) / jnp.sqrt(jnp.float32(C * BH * BW))

    def mlp_block(carry, index):
        grad_one, grad_two, grad_three = carry
        x_flat = lax.dynamic_slice_in_dim(inputs, index * BH, BH, 1).reshape(C, BH * WCOL)
        dy_flat = lax.dynamic_slice_in_dim(dy, index * BH, BH, 1).reshape(C, BH * WCOL)
        pre_act = jnp.dot(w_in.T, x_flat, preferred_element_type=jnp.float32) + bias_in[:, None]
        sigma = jax.nn.sigmoid(pre_act)
        act = (pre_act * sigma).astype(jnp.bfloat16)
        dact = jnp.dot(w_out, dy_flat, preferred_element_type=jnp.float32)
        dpre = (dact * sigma * (1.0 + pre_act * (1.0 - sigma))).astype(jnp.bfloat16)
        dx_flat = dy_flat.astype(jnp.float32) + jnp.dot(w_in, dpre, preferred_element_type=jnp.float32)
        grad_one = grad_one + jnp.dot(x_flat, dpre.T, preferred_element_type=jnp.float32)
        grad_two = grad_two + lax.optimization_barrier(jnp.sum(dpre.astype(jnp.float32), axis=1))
        grad_three = grad_three + jnp.dot(act, dy_flat.T, preferred_element_type=jnp.float32)
        return ((grad_one, grad_two, grad_three), dx_flat.astype(jnp.bfloat16).reshape(C, BH, WCOL))
    start = (jnp.zeros((C, HID), jnp.float32), jnp.zeros((HID,), jnp.float32), jnp.zeros((HID, C), jnp.float32))
    sums, dx_blocks = lax.scan(mlp_block, start, jnp.arange(NROWS // BH, dtype=jnp.int32))
    grad_inputs = dx_blocks.transpose(1, 0, 2, 3).reshape(C, NROWS, WCOL)
    scale = 1.0 / jnp.sqrt(jnp.float32(NROWS * WCOL))
    return (grad_inputs, sums[0] * scale, sums[1] * scale, sums[2] * scale, grad_frac)
```

```python
import math

import jax
import jax.numpy as jnp
import numpy as np
from jax import lax
from jax.experimental import pallas as pl
from jax.experimental.pallas import tpu as pltpu
from jax.sharding import PartitionSpec as P

C = 256
BH = 16
BW = 256
LANES = 128
VMEM_BYTES = 48 * 1024 * 1024


def extended_2(cells, sides, width):
    for axis, dim in sides:
        count = lax.axis_size(axis)
        ends = count - 1
        head = lax.slice_in_dim(cells, 0, width, axis=dim)
        tail = lax.slice_in_dim(cells, cells.shape[dim] - width, cells.shape[dim], axis=dim)
        cells = jnp.concatenate(
            [
                lax.ppermute(tail, axis, [(i, (i + 1) % count) for i in range(ends)]),
                cells,
                lax.ppermute(head, axis, [((i + 1) % count, i) for i in range(ends)]),
            ],
            axis=dim,
        )
    return cells


def from_behind(block, axis, distance):
    devices = range(lax.axis_size(axis))
    route = [(i - distance, i) for i in devices if i - distance in devices]
    return lax.ppermute(block, axis, route)


def catmull(frac):
    square = frac * frac
    cube = square * frac
    weights = (
        0.5 * (-cube + 2.0 * square - frac),
        0.5 * (3.0 * cube - 5.0 * square + 2.0),
        0.5 * (-3.0 * cube + 4.0 * square + frac),
        0.5 * (cube - square),
    )
    slopes = (
        0.5 * (-3.0 * square + 4.0 * frac - 1.0),
        0.5 * (9.0 * square - 10.0 * frac),
        0.5 * (-9.0 * square + 8.0 * frac + 1.0),
        0.5 * (3.0 * square - 2.0 * frac),
    )
    return (weights, slopes)


def band_matrix(position, frac, inner):
    offset_grid = (
        jnp.arange(3 * inner, dtype=jnp.int32)[None, None, :]
        - jnp.arange(inner, dtype=jnp.int32)[None, :, None]
        - position[:, None, None]
    )
    weights, slopes = catmull(frac)
    value = jnp.zeros(offset_grid.shape, jnp.float32)
    slope = jnp.zeros(offset_grid.shape, jnp.float32)
    for tap in range(4):
        value = value + jnp.where(offset_grid == tap, weights[tap][:, None, None], 0.0)
        slope = slope + jnp.where(offset_grid == tap, slopes[tap][:, None, None], 0.0)
    return (value.astype(jnp.bfloat16), slope.astype(jnp.bfloat16))


def contract_points(left, right):
    return lax.dot_general(
        left, right, (((1,), (1,)), ((), ())), preferred_element_type=jnp.float32
    )


def shards(
    inputs, w_in, bias_in, w_out, advected, cotangent, offsets, stencil_row, stencil_col, fracs
):
    channels_dev, band_rows, columns = advected.shape
    row_blocks = band_rows // BH
    blocks = columns // BW
    point_rows = inputs.shape[1]
    x_flat = inputs.reshape(C, point_rows * columns)
    pre_act = (
        lax.dot_general(w_in, x_flat, (((0,), (0,)), ((), ())), preferred_element_type=jnp.float32)
        + bias_in[:, None]
    )
    sigma = jax.nn.sigmoid(pre_act)
    act = (pre_act * sigma).astype(jnp.bfloat16)
    padded = extended_2(advected, (("lat", 1),), BH)
    row_pos = BH // 2 * offsets[0] + stencil_row
    col_pos = BW // 2 * offsets[1] + stencil_col

    def per_row(index, state):
        extended, frac_acc = state
        drow = lax.dynamic_slice_in_dim(cotangent, index * BH, BH, 1)
        window = lax.dynamic_slice_in_dim(padded, index * BH, 3 * BH, 1)
        ry_value, ry_slope = band_matrix(row_pos[index], fracs[0][index], BH)
        rx_value, rx_slope = band_matrix(col_pos[index], fracs[1][index], BW)
        column_sums = [
            jnp.zeros((channels_dev, 3 * BH, BW), jnp.float32) for unused in range(blocks)
        ]
        grad_rows = []
        grad_cols = []
        for block in range(blocks):
            left = (block - 1) % blocks
            right = (block + 1) % blocks
            rx_both = jnp.concatenate([rx_value[block], rx_slope[block]], axis=1)
            block_cot = drow[:, :, block * BW : (block + 1) * BW].reshape(channels_dev * BH, BW)
            product = jnp.dot(block_cot, rx_both, preferred_element_type=jnp.float32)
            product = product.reshape(channels_dev, BH, 6 * BW)
            z_value = product[:, :, : 3 * BW]
            z_slope = product[:, :, 3 * BW :]
            ry_value_all = jnp.broadcast_to(ry_value[block], (channels_dev, BH, 3 * BH))
            ry_slope_all = jnp.broadcast_to(ry_slope[block], (channels_dev, BH, 3 * BH))
            spread = jnp.einsum(
                "cho,chv->cov",
                ry_value_all,
                z_value.astype(jnp.bfloat16),
                preferred_element_type=jnp.float32,
            )
            source = jnp.concatenate(
                [
                    window[:, :, left * BW : (left + 1) * BW],
                    window[:, :, block * BW : (block + 1) * BW],
                    window[:, :, right * BW : (right + 1) * BW],
                ],
                axis=2,
            )
            ry_both = jnp.concatenate([ry_value_all, ry_slope_all], axis=1)
            lifted = jnp.einsum("cjo,cov->cjv", ry_both, source, preferred_element_type=jnp.float32)
            grad_rows.append(jnp.sum(lifted[:, BH:] * z_value))
            grad_cols.append(jnp.sum(lifted[:, :BH] * z_slope))
            for part, target in ((0, left), (1, block), (2, right)):
                column_sums[target] = (
                    column_sums[target] + spread[:, :, part * BW : (part + 1) * BW]
                )
        row_sum = jnp.concatenate(column_sums, axis=2)
        current = lax.dynamic_slice_in_dim(extended, index * BH, 3 * BH, 1)
        extended = lax.dynamic_update_slice_in_dim(extended, current + row_sum, index * BH, 1)
        frac_acc = frac_acc.at[:, index].set(
            jnp.stack([jnp.stack(grad_rows), jnp.stack(grad_cols)])
        )
        return (extended, frac_acc)

    start_field = jnp.zeros((channels_dev, band_rows + 2 * BH, columns), jnp.float32)
    start_frac = jnp.zeros((2, row_blocks, blocks), jnp.float32)
    extended, frac_local = lax.fori_loop(0, row_blocks, per_row, (start_field, start_frac))
    from_below = from_behind(extended[:, :BH], "lat", -1)
    from_above = from_behind(extended[:, band_rows + BH :], "lat", 1)
    inner_rows = jnp.concatenate(
        [
            extended[:, BH : 2 * BH] + from_above,
            extended[:, 2 * BH : band_rows],
            extended[:, band_rows : band_rows + BH] + from_below,
        ],
        axis=1,
    )
    dy_band = inner_rows.astype(jnp.bfloat16)
    dy_points = lax.all_to_all(dy_band, "grp", split_axis=1, concat_axis=0, tiled=True)
    dy_flat = dy_points.reshape(C, point_rows * columns)
    dact = jnp.dot(w_out, dy_flat, preferred_element_type=jnp.float32)
    frac_total = lax.psum(frac_local, "grp")
    grad_frac = frac_total / math.sqrt(C * BH * BW)
    dpre = (dact * sigma * (1.0 + pre_act * (1.0 - sigma))).astype(jnp.bfloat16)
    dx_flat = dy_flat.astype(jnp.float32) + jnp.dot(w_in, dpre, preferred_element_type=jnp.float32)
    grad_inputs = dx_flat.astype(jnp.bfloat16).reshape(C, point_rows, columns)
    grad_first = contract_points(x_flat, dpre)
    grad_shift = jnp.sum(dpre.astype(jnp.float32), axis=1)
    grad_second = contract_points(act, dy_flat)
    total_points = point_rows * columns * lax.axis_size("lat") * lax.axis_size("grp")
    scale = 1.0 / math.sqrt(total_points)
    banded = (
        lax.psum_scatter(grad_first, "lat", scatter_dimension=1, tiled=True),
        lax.psum_scatter(grad_shift, "lat", scatter_dimension=0, tiled=True),
        lax.psum_scatter(grad_second, "lat", scatter_dimension=0, tiled=True),
    )
    summed = (
        lax.psum_scatter(banded[0], "grp", scatter_dimension=1, tiled=True),
        lax.psum_scatter(banded[1], "grp", scatter_dimension=0, tiled=True),
        lax.psum_scatter(banded[2], "grp", scatter_dimension=0, tiled=True),
    )
    return (grad_inputs, summed[0] * scale, summed[1] * scale, summed[2] * scale, grad_frac)


def taps(grid, values):
    out = jnp.zeros(grid.shape, jnp.float32)
    for tap in range(4):
        out = jnp.where(grid == tap, values[tap], out)
    return out.astype(jnp.bfloat16)


def column_grid():
    shape = (BW, BW + LANES)
    return lax.broadcasted_iota(jnp.int32, shape, 1) - lax.broadcasted_iota(jnp.int32, shape, 0)


def spread_kernel(
    ints, floats, cot_ref, top_ref, bottom_ref, grid_ref, even_ref, odd_ref, acc, held
):
    step = pl.program_id(0)
    steps = pl.num_programs(0)
    channels, unused, columns = held.shape
    blocks = columns // BW
    group = grid_ref.shape[1] // BH

    @pl.when(step == 0)
    def first():
        acc[...] = jnp.zeros_like(acc)
        held[...] = top_ref[...]

    @pl.when(step == steps - 1)
    def last():
        held[...] = bottom_ref[...]

    @pl.when((step > 0) & (step < steps - 1))
    def inner():
        held[...] = cot_ref[...]

    for block in range(blocks):
        place = (step * blocks + block) * 4
        weight = (step * blocks + block) * 16
        row_off, row_st, col_off, col_st = [ints[place + k] for k in range(4)]
        rx = taps(column_grid() - col_st, [floats[weight + 8 + k] for k in range(4)])
        ry = taps(grid_ref[...] - row_st, [floats[weight + k] for k in range(4)])
        piece = held[:, :, block * BW : (block + 1) * BW].reshape(channels * BH, BW)
        z = jnp.dot(piece, rx, preferred_element_type=jnp.float32).astype(jnp.bfloat16)
        rows = pl.ds(pl.multiple_of(row_off * 8, 8), 3 * BH // 2)
        cols = pl.ds(pl.multiple_of((col_off + 2 * block) * LANES, LANES), BW + LANES)
        for part in range(channels // group):
            spread = jnp.dot(
                ry,
                z[part * group * BH : (part + 1) * group * BH],
                preferred_element_type=jnp.float32,
            ).reshape(group, 3 * BH // 2, BW + LANES)
            where = (slice(part * group, (part + 1) * group), rows, cols)
            acc[where] = acc[where] + spread

    def finished():
        left = acc[:, :BH, BW : 2 * BW] + acc[:, :BH, columns + BW :]
        right = acc[:, :BH, columns : columns + BW] + acc[:, :BH, :BW]
        middle = acc[:, :BH, 2 * BW : columns]
        whole = jnp.concatenate([left, middle, right], axis=2)
        return jnp.swapaxes(whole, 0, 1).astype(jnp.bfloat16)[None]

    @pl.when((step >= 2) & (step % 2 == 0))
    def even():
        even_ref[...] = finished()

    @pl.when((step >= 2) & (step % 2 == 1))
    def odd():
        odd_ref[...] = finished()

    acc[:, :BH] = acc[:, BH : 2 * BH]
    acc[:, BH : 2 * BH] = acc[:, 2 * BH :]
    acc[:, 2 * BH :] = jnp.zeros((channels, BH, acc.shape[2]), jnp.float32)


def spread_call(ints, floats, cotangent, top, bottom, half, halves):
    channels, band_rows, columns = cotangent.shape
    part = channels // halves
    row_blocks = band_rows // BH
    group = 8
    across = np.arange(group * 3 * BH // 2)[:, None]
    along = np.arange(group * BH)[None, :]
    same = across // (3 * BH // 2) == along // BH
    grid = np.where(same, across % (3 * BH // 2) - along % BH, -1000).astype(np.int32)
    halo = pl.BlockSpec((part, BH, columns), lambda i, *s: (half, 0, 0))
    result = jax.ShapeDtypeStruct((row_blocks // 2, BH, part, columns), jnp.bfloat16)
    out_spec = pl.BlockSpec(
        (1, BH, part, columns), lambda i, *s: (jnp.maximum(i - 2, 0) // 2, 0, 0, 0)
    )
    flops = 2 * (row_blocks + 2) * (columns // BW) * part * BH * (BW + LANES) * (BW + 8 * 24)
    return pl.pallas_call(
        spread_kernel,
        grid_spec=pltpu.PrefetchScalarGridSpec(
            num_scalar_prefetch=2,
            grid=(row_blocks + 2,),
            in_specs=[
                pl.BlockSpec(
                    (part, BH, columns),
                    lambda i, *s: (half, jnp.clip(i - 1, 0, row_blocks - 1), 0),
                ),
                halo,
                halo,
                pl.BlockSpec(grid.shape, lambda i, *s: (0, 0)),
            ],
            out_specs=[out_spec, out_spec],
            scratch_shapes=[
                pltpu.VMEM((part, 3 * BH, columns + 2 * BW), jnp.float32),
                pltpu.VMEM((part, BH, columns), jnp.bfloat16),
            ],
        ),
        out_shape=[result, result],
        compiler_params=pltpu.CompilerParams(vmem_limit_bytes=VMEM_BYTES),
        cost_estimate=pl.CostEstimate(
            flops=flops, bytes_accessed=4 * part * band_rows * columns, transcendentals=0
        ),
        name="spread",
    )(ints, floats, cotangent, top, bottom, jnp.asarray(grid))


def frac_kernel(
    ints, floats, cot_ref, before_ref, here_ref, after_ref, top_ref, bottom_ref, grid_ref,
    out_ref, window, rx_both, ry_both
):
    step = pl.program_id(0)
    steps = pl.num_programs(0)
    channels, unused, columns = cot_ref.shape
    blocks = columns // BW
    group = grid_ref.shape[0] // BH

    def fill(rows, ref):
        window[:, rows, BW : columns + BW] = ref[...]
        window[:, rows, :BW] = ref[:, :, columns - BW :]
        window[:, rows, columns + BW :] = ref[:, :, :BW]

    @pl.when(step == 0)
    def first():
        fill(slice(0, BH), top_ref)

    @pl.when(step > 0)
    def before():
        fill(slice(0, BH), before_ref)

    fill(slice(BH, 2 * BH), here_ref)

    @pl.when(step == steps - 1)
    def last():
        fill(slice(2 * BH, 3 * BH), bottom_ref)

    @pl.when(step < steps - 1)
    def after():
        fill(slice(2 * BH, 3 * BH), after_ref)

    @pl.when(pl.program_id(1) == 0)
    def matrices():
        out_ref[...] = jnp.zeros_like(out_ref)
        for block in range(blocks):
            place = ((step + 1) * blocks + block) * 4
            weight = ((step + 1) * blocks + block) * 16
            row_off, row_st, unused_off, col_st = [ints[place + k] for k in range(4)]
            row_grid = grid_ref[...] - (row_off * 8 + row_st)
            ry_both[block, : group * BH] = taps(row_grid, [floats[weight + k] for k in range(4)])
            ry_both[block, group * BH :] = taps(
                row_grid, [floats[weight + 4 + k] for k in range(4)]
            )
            col_grid = column_grid() - col_st
            rx_both[block, :, : BW + LANES] = taps(
                col_grid, [floats[weight + 8 + k] for k in range(4)]
            )
            rx_both[block, :, BW + LANES :] = taps(
                col_grid, [floats[weight + 12 + k] for k in range(4)]
            )

    for block in range(blocks):
        col_off = ints[((step + 1) * blocks + block) * 4 + 2]
        cols = pl.ds(pl.multiple_of((col_off + 2 * block) * LANES, LANES), BW + LANES)
        piece = cot_ref[:, :, block * BW : (block + 1) * BW].reshape(channels * BH, BW)
        z = jnp.dot(piece, rx_both[block], preferred_element_type=jnp.float32)
        row_total = jnp.zeros((1, BW + LANES), jnp.float32)
        col_total = jnp.zeros((1, BW + LANES), jnp.float32)
        for part in range(channels // group):
            source = window[part * group : (part + 1) * group, :, cols]
            source = source.reshape(group * 3 * BH, BW + LANES)
            lifted = jnp.dot(ry_both[block], source, preferred_element_type=jnp.float32)
            zs = z[part * group * BH : (part + 1) * group * BH]
            row_total += jnp.sum(
                lifted[group * BH :] * zs[:, : BW + LANES], axis=0, keepdims=True
            )
            col_total += jnp.sum(
                lifted[: group * BH] * zs[:, BW + LANES :], axis=0, keepdims=True
            )
        out_ref[0, block : block + 1] += row_total
        out_ref[0, blocks + block : blocks + block + 1] += col_total


def frac_call(ints, floats, cotangent, advected, top, bottom):
    channels, band_rows, columns = cotangent.shape
    part = 16
    row_blocks = band_rows // BH
    blocks = columns // BW
    group = 8
    across = np.arange(group * BH)[:, None]
    along = np.arange(group * 3 * BH)[None, :]
    same = across // BH == along // (3 * BH)
    grid = np.where(same, along % (3 * BH) - across % BH, -1000).astype(np.int32)

    def rows(shift):
        return pl.BlockSpec(
            (part, BH, columns),
            lambda i, c, *s: (c, jnp.clip(i + shift, 0, row_blocks - 1), 0),
        )

    halo = pl.BlockSpec((part, BH, columns), lambda i, c, *s: (c, 0, 0))
    flops = 2 * row_blocks * blocks * channels * BH * (BW + LANES) * (2 * BW + 2 * group * 3 * BH)
    return pl.pallas_call(
        frac_kernel,
        grid_spec=pltpu.PrefetchScalarGridSpec(
            num_scalar_prefetch=2,
            grid=(row_blocks, channels // part),
            in_specs=[
                rows(0),
                rows(-1),
                rows(0),
                rows(1),
                halo,
                halo,
                pl.BlockSpec(grid.shape, lambda i, c, *s: (0, 0)),
            ],
            out_specs=pl.BlockSpec((1, 2 * blocks, BW + LANES), lambda i, c, *s: (i, 0, 0)),
            scratch_shapes=[
                pltpu.VMEM((part, 3 * BH, columns + 2 * BW), jnp.bfloat16),
                pltpu.VMEM((blocks, BW, 2 * (BW + LANES)), jnp.bfloat16),
                pltpu.VMEM((blocks, 2 * group * BH, group * 3 * BH), jnp.bfloat16),
            ],
        ),
        out_shape=jax.ShapeDtypeStruct((row_blocks, 2 * blocks, BW + LANES), jnp.float32),
        compiler_params=pltpu.CompilerParams(vmem_limit_bytes=VMEM_BYTES),
        cost_estimate=pl.CostEstimate(
            flops=flops, bytes_accessed=8 * channels * band_rows * columns, transcendentals=0
        ),
        name="frac",
    )(ints, floats, cotangent, advected, advected, advected, top, bottom, jnp.asarray(grid))


def mlp_kernel(*refs):
    x_ref, dy0_ref, dy1_ref, w_in_ref, w_in_t_ref, bias_ref, w_out_ref = refs[:7]
    dx_ref, first_ref, shift_ref, second_ref, x_flat, dy_flat, dx_rows = refs[-7:]
    width = x_ref.shape[2]

    @pl.when(pl.program_id(0) == 0)
    def clear():
        first_ref[...] = jnp.zeros_like(first_ref)
        shift_ref[...] = jnp.zeros_like(shift_ref)
        second_ref[...] = jnp.zeros_like(second_ref)

    x_rows = jnp.swapaxes(x_ref[...].astype(jnp.float32), 0, 1).astype(jnp.bfloat16)
    for row in range(BH):
        cols = slice(row * width, (row + 1) * width)
        x_flat[:, cols] = x_rows[row]
        dy_flat[:, 0, :, cols] = dy0_ref[:, row]
        dy_flat[:, 1, :, cols] = dy1_ref[:, row]
    tile = 1024
    for start in range(0, BH * width, tile):
        cols = slice(start, start + tile)
        x = x_flat[:, cols]
        dy = dy_flat[:, :, :, cols].reshape(x.shape)
        pre = jnp.dot(w_in_t_ref[...], x, preferred_element_type=jnp.float32) + bias_ref[...]
        sigma = jax.nn.sigmoid(pre)
        act = (pre * sigma).astype(jnp.bfloat16)
        dact = jnp.dot(w_out_ref[...], dy, preferred_element_type=jnp.float32)
        dpre_wide = dact * sigma * (1.0 + pre * (1.0 - sigma))
        dpre = dpre_wide.astype(jnp.bfloat16)
        dx = dy.astype(jnp.float32) + jnp.dot(
            w_in_ref[...], dpre, preferred_element_type=jnp.float32
        )
        for part in range(tile // width):
            dx_rows[start // width + part] = dx[:, part * width : (part + 1) * width]
        first_ref[...] += contract_points(x, dpre)
        second_ref[...] += contract_points(act, dy)
        shift_ref[...] += jnp.sum(dpre.astype(jnp.float32), axis=1, keepdims=True)
    dx_ref[...] = jnp.swapaxes(dx_rows[...], 0, 1).astype(jnp.bfloat16)


def mlp_call(inputs, dy0, dy1, w_in, bias_in, w_out, half, earlier):
    channels, point_rows, columns = inputs.shape
    hidden = w_in.shape[1]
    sources, unused, part, unused_columns = dy0.shape
    width = LANES
    whole = lambda shape: pl.BlockSpec(shape, lambda j: (0, 0))
    points = pl.BlockSpec((channels, BH, width), lambda j: (0, half, j))
    dy_spec = pl.BlockSpec((sources, BH, part, width), lambda j: (0, 0, 0, j))
    operands = [inputs, dy0, dy1, w_in, w_in.T, bias_in[:, None], w_out]
    in_specs = [
        points,
        dy_spec,
        dy_spec,
        whole((channels, hidden)),
        whole((hidden, channels)),
        whole((hidden, 1)),
        whole((hidden, channels)),
    ]
    aliases = {}
    if earlier is not None:
        operands.append(earlier)
        in_specs.append(pl.BlockSpec(memory_space=pl.ANY))
        aliases = {7: 0}
    return pl.pallas_call(
        mlp_kernel,
        grid=(columns // width,),
        in_specs=in_specs,
        out_specs=[
            points,
            whole((channels, hidden)),
            whole((hidden, 1)),
            whole((hidden, channels)),
        ],
        out_shape=[
            jax.ShapeDtypeStruct(inputs.shape, jnp.bfloat16),
            jax.ShapeDtypeStruct((channels, hidden), jnp.float32),
            jax.ShapeDtypeStruct((hidden, 1), jnp.float32),
            jax.ShapeDtypeStruct((hidden, channels), jnp.float32),
        ],
        scratch_shapes=[
            pltpu.VMEM((channels, BH * width), jnp.bfloat16),
            pltpu.VMEM((sources, 2, part, BH * width), jnp.bfloat16),
            pltpu.VMEM((BH, channels, width), jnp.float32),
        ],
        input_output_aliases=aliases,
        compiler_params=pltpu.CompilerParams(vmem_limit_bytes=VMEM_BYTES),
        cost_estimate=pl.CostEstimate(
            flops=10 * channels * hidden * BH * columns,
            bytes_accessed=6 * channels * BH * columns,
            transcendentals=2 * hidden * BH * columns,
        ),
        name="mlp",
    )(*operands)


def scattered(grid, axis):
    count = lax.axis_size(axis)
    parts = grid.reshape((count, grid.shape[0] // count) + grid.shape[1:])
    return jnp.sum(lax.all_to_all(parts, axis, split_axis=0, concat_axis=0, tiled=True), axis=0)


def neighbours(cells, axis, dim, width):
    count = lax.axis_size(axis)
    ends = count - 1
    head = lax.slice_in_dim(cells, 0, width, axis=dim)
    tail = lax.slice_in_dim(cells, cells.shape[dim] - width, cells.shape[dim], axis=dim)
    return (
        lax.ppermute(tail, axis, [(i, i + 1) for i in range(ends)]),
        lax.ppermute(head, axis, [(i + 1, i) for i in range(ends)]),
    )


def fast_shards(
    inputs, w_in, bias_in, w_out, advected, cotangent, offsets, stencil_row, stencil_col, fracs
):
    band_rows, columns = advected.shape[1:]
    hidden = w_in.shape[1]
    blocks = columns // BW
    row_blocks = band_rows // BH
    places = jnp.stack([offsets[0], stencil_row, offsets[1], stencil_col], axis=-1)
    table = jnp.concatenate([places.astype(jnp.float32), jnp.moveaxis(fracs, 0, -1)], axis=-1)
    above, below = neighbours(table, "lat", 0, 1)
    table = jnp.concatenate([above, table, below], axis=0)
    ints = table[..., :4].astype(jnp.int32).reshape(-1)
    row_w, row_s = catmull(table[..., 4])
    col_w, col_s = catmull(table[..., 5])
    floats = jnp.stack([*row_w, *row_s, *col_w, *col_s], axis=-1).reshape(-1)

    cot_top, cot_bottom = neighbours(cotangent, "lat", 1, BH)

    def to_points(cells):
        return lax.all_to_all(cells, "grp", split_axis=0, concat_axis=0, tiled=True)

    even0, odd0 = spread_call(ints, floats, cotangent, cot_top, cot_bottom, 0, 2)
    dy_even0 = to_points(even0)
    even1, odd1 = spread_call(ints, floats, cotangent, cot_top, cot_bottom, 1, 2)
    dy_even1 = to_points(even1)
    odd0, dy_even0 = lax.optimization_barrier((odd0, dy_even0))
    dy_odd0 = to_points(odd0)
    odd1, dy_even1 = lax.optimization_barrier((odd1, dy_even1))
    dy_odd1 = to_points(odd1)

    adv_top, adv_bottom = neighbours(advected, "lat", 1, BH)
    frac_parts = frac_call(ints, floats, cotangent, advected, adv_top, adv_bottom)
    frac_local = jnp.sum(frac_parts, axis=2).reshape(row_blocks, 2, blocks)
    frac_total = lax.psum(jnp.moveaxis(frac_local, 1, 0), "grp")
    grad_frac = frac_total / math.sqrt(C * BH * BW)

    early = mlp_call(inputs, dy_even0, dy_even1, w_in, bias_in, w_out, 0, None)
    late = mlp_call(inputs, dy_odd0, dy_odd1, w_in, bias_in, w_out, 1, early[0])
    first, shift, second = [early[k] + late[k] for k in (1, 2, 3)]
    merged = jnp.concatenate([first.T, second, jnp.broadcast_to(shift, (hidden, LANES))], axis=1)
    share = scattered(scattered(merged, "lat"), "grp")
    total_points = band_rows * columns * lax.axis_size("lat")
    share = share * (1.0 / math.sqrt(total_points))
    return (late[0], share[:, :C].T, share[:, 2 * C], share[:, C : 2 * C], grad_frac)


def solution(mesh):
    grp = mesh.shape["grp"]

    def chosen(*args):
        band_rows = args[4].shape[1]
        channels = args[4].shape[0]
        paired = args[0].shape[1] == 2 * BH and band_rows == 2 * BH * grp
        return (fast_shards if paired and channels % 32 == 0 else shards)(*args)

    placed = (
        P(None, ("lat", "grp"), None),
        P(),
        P(),
        P(),
        P("grp", "lat", None),
        P("grp", "lat", None),
        P(None, "lat", None),
        P("lat", None),
        P("lat", None),
        P(None, "lat", None),
    )
    return jax.shard_map(
        chosen,
        mesh=mesh,
        in_specs=placed,
        out_specs=(
            P(None, ("lat", "grp"), None),
            P(None, ("lat", "grp")),
            P(("lat", "grp")),
            P(("lat", "grp"), None),
            P(None, "lat", None),
        ),
        check_vma=False,
    )
```

```python
import math

import jax
import jax.numpy as jnp
import numpy as np
from jax import lax
from jax.experimental import pallas as pl
from jax.experimental.pallas import tpu as pltpu
from jax.sharding import PartitionSpec as P

C = 256
BH = 16
BW = 256
LANES = 128
VMEM_BYTES = 48 * 1024 * 1024


def extended_2(cells, sides, width):
    for axis, dim in sides:
        count = lax.axis_size(axis)
        ends = count - 1
        head = lax.slice_in_dim(cells, 0, width, axis=dim)
        tail = lax.slice_in_dim(cells, cells.shape[dim] - width, cells.shape[dim], axis=dim)
        cells = jnp.concatenate(
            [
                lax.ppermute(tail, axis, [(i, (i + 1) % count) for i in range(ends)]),
                cells,
                lax.ppermute(head, axis, [((i + 1) % count, i) for i in range(ends)]),
            ],
            axis=dim,
        )
    return cells


def from_behind(block, axis, distance):
    devices = range(lax.axis_size(axis))
    route = [(i - distance, i) for i in devices if i - distance in devices]
    return lax.ppermute(block, axis, route)


def catmull(frac):
    square = frac * frac
    cube = square * frac
    weights = (
        0.5 * (-cube + 2.0 * square - frac),
        0.5 * (3.0 * cube - 5.0 * square + 2.0),
        0.5 * (-3.0 * cube + 4.0 * square + frac),
        0.5 * (cube - square),
    )
    slopes = (
        0.5 * (-3.0 * square + 4.0 * frac - 1.0),
        0.5 * (9.0 * square - 10.0 * frac),
        0.5 * (-9.0 * square + 8.0 * frac + 1.0),
        0.5 * (3.0 * square - 2.0 * frac),
    )
    return (weights, slopes)


def band_matrix(position, frac, inner):
    offset_grid = (
        jnp.arange(3 * inner, dtype=jnp.int32)[None, None, :]
        - jnp.arange(inner, dtype=jnp.int32)[None, :, None]
        - position[:, None, None]
    )
    weights, slopes = catmull(frac)
    value = jnp.zeros(offset_grid.shape, jnp.float32)
    slope = jnp.zeros(offset_grid.shape, jnp.float32)
    for tap in range(4):
        value = value + jnp.where(offset_grid == tap, weights[tap][:, None, None], 0.0)
        slope = slope + jnp.where(offset_grid == tap, slopes[tap][:, None, None], 0.0)
    return (value.astype(jnp.bfloat16), slope.astype(jnp.bfloat16))


def contract_points(left, right):
    return lax.dot_general(
        left, right, (((1,), (1,)), ((), ())), preferred_element_type=jnp.float32
    )


def shards(
    inputs, w_in, bias_in, w_out, advected, cotangent, offsets, stencil_row, stencil_col, fracs
):
    channels_dev, band_rows, columns = advected.shape
    row_blocks = band_rows // BH
    blocks = columns // BW
    point_rows = inputs.shape[1]
    x_flat = inputs.reshape(C, point_rows * columns)
    pre_act = (
        lax.dot_general(w_in, x_flat, (((0,), (0,)), ((), ())), preferred_element_type=jnp.float32)
        + bias_in[:, None]
    )
    sigma = jax.nn.sigmoid(pre_act)
    act = (pre_act * sigma).astype(jnp.bfloat16)
    padded = extended_2(advected, (("lat", 1),), BH)
    row_pos = BH // 2 * offsets[0] + stencil_row
    col_pos = BW // 2 * offsets[1] + stencil_col

    def per_row(index, state):
        extended, frac_acc = state
        drow = lax.dynamic_slice_in_dim(cotangent, index * BH, BH, 1)
        window = lax.dynamic_slice_in_dim(padded, index * BH, 3 * BH, 1)
        ry_value, ry_slope = band_matrix(row_pos[index], fracs[0][index], BH)
        rx_value, rx_slope = band_matrix(col_pos[index], fracs[1][index], BW)
        column_sums = [
            jnp.zeros((channels_dev, 3 * BH, BW), jnp.float32) for unused in range(blocks)
        ]
        grad_rows = []
        grad_cols = []
        for block in range(blocks):
            left = (block - 1) % blocks
            right = (block + 1) % blocks
            rx_both = jnp.concatenate([rx_value[block], rx_slope[block]], axis=1)
            block_cot = drow[:, :, block * BW : (block + 1) * BW].reshape(channels_dev * BH, BW)
            product = jnp.dot(block_cot, rx_both, preferred_element_type=jnp.float32)
            product = product.reshape(channels_dev, BH, 6 * BW)
            z_value = product[:, :, : 3 * BW]
            z_slope = product[:, :, 3 * BW :]
            ry_value_all = jnp.broadcast_to(ry_value[block], (channels_dev, BH, 3 * BH))
            ry_slope_all = jnp.broadcast_to(ry_slope[block], (channels_dev, BH, 3 * BH))
            spread = jnp.einsum(
                "cho,chv->cov",
                ry_value_all,
                z_value.astype(jnp.bfloat16),
                preferred_element_type=jnp.float32,
            )
            source = jnp.concatenate(
                [
                    window[:, :, left * BW : (left + 1) * BW],
                    window[:, :, block * BW : (block + 1) * BW],
                    window[:, :, right * BW : (right + 1) * BW],
                ],
                axis=2,
            )
            ry_both = jnp.concatenate([ry_value_all, ry_slope_all], axis=1)
            lifted = jnp.einsum("cjo,cov->cjv", ry_both, source, preferred_element_type=jnp.float32)
            grad_rows.append(jnp.sum(lifted[:, BH:] * z_value))
            grad_cols.append(jnp.sum(lifted[:, :BH] * z_slope))
            for part, target in ((0, left), (1, block), (2, right)):
                column_sums[target] = (
                    column_sums[target] + spread[:, :, part * BW : (part + 1) * BW]
                )
        row_sum = jnp.concatenate(column_sums, axis=2)
        current = lax.dynamic_slice_in_dim(extended, index * BH, 3 * BH, 1)
        extended = lax.dynamic_update_slice_in_dim(extended, current + row_sum, index * BH, 1)
        frac_acc = frac_acc.at[:, index].set(
            jnp.stack([jnp.stack(grad_rows), jnp.stack(grad_cols)])
        )
        return (extended, frac_acc)

    start_field = jnp.zeros((channels_dev, band_rows + 2 * BH, columns), jnp.float32)
    start_frac = jnp.zeros((2, row_blocks, blocks), jnp.float32)
    extended, frac_local = lax.fori_loop(0, row_blocks, per_row, (start_field, start_frac))
    from_below = from_behind(extended[:, :BH], "lat", -1)
    from_above = from_behind(extended[:, band_rows + BH :], "lat", 1)
    inner_rows = jnp.concatenate(
        [
            extended[:, BH : 2 * BH] + from_above,
            extended[:, 2 * BH : band_rows],
            extended[:, band_rows : band_rows + BH] + from_below,
        ],
        axis=1,
    )
    dy_band = inner_rows.astype(jnp.bfloat16)
    dy_points = lax.all_to_all(dy_band, "grp", split_axis=1, concat_axis=0, tiled=True)
    dy_flat = dy_points.reshape(C, point_rows * columns)
    dact = jnp.dot(w_out, dy_flat, preferred_element_type=jnp.float32)
    frac_total = lax.psum(frac_local, "grp")
    grad_frac = frac_total / math.sqrt(C * BH * BW)
    dpre = (dact * sigma * (1.0 + pre_act * (1.0 - sigma))).astype(jnp.bfloat16)
    dx_flat = dy_flat.astype(jnp.float32) + jnp.dot(w_in, dpre, preferred_element_type=jnp.float32)
    grad_inputs = dx_flat.astype(jnp.bfloat16).reshape(C, point_rows, columns)
    grad_first = contract_points(x_flat, dpre)
    grad_shift = jnp.sum(dpre.astype(jnp.float32), axis=1)
    grad_second = contract_points(act, dy_flat)
    total_points = point_rows * columns * lax.axis_size("lat") * lax.axis_size("grp")
    scale = 1.0 / math.sqrt(total_points)
    banded = (
        lax.psum_scatter(grad_first, "lat", scatter_dimension=1, tiled=True),
        lax.psum_scatter(grad_shift, "lat", scatter_dimension=0, tiled=True),
        lax.psum_scatter(grad_second, "lat", scatter_dimension=0, tiled=True),
    )
    summed = (
        lax.psum_scatter(banded[0], "grp", scatter_dimension=1, tiled=True),
        lax.psum_scatter(banded[1], "grp", scatter_dimension=0, tiled=True),
        lax.psum_scatter(banded[2], "grp", scatter_dimension=0, tiled=True),
    )
    return (grad_inputs, summed[0] * scale, summed[1] * scale, summed[2] * scale, grad_frac)


def taps(grid, values):
    out = jnp.zeros(grid.shape, jnp.float32)
    for tap in range(4):
        out = jnp.where(grid == tap, values[tap], out)
    return out.astype(jnp.bfloat16)


def column_matrix(position, values):
    shape = (BW // 2, BW)
    grid = lax.broadcasted_iota(jnp.int32, shape, 1) - lax.broadcasted_iota(jnp.int32, shape, 0)
    corner = taps(grid - position, values)
    empty = jnp.zeros((BW // 2, LANES), jnp.bfloat16)
    upper = jnp.concatenate([corner, empty], axis=1)
    lower = jnp.concatenate([empty, corner], axis=1)
    return jnp.concatenate([upper, lower], axis=0)


def spread_kernel(
    ints, floats, cot_ref, top_ref, bottom_ref, grid_ref, even_ref, odd_ref, acc, held
):
    step = pl.program_id(0)
    steps = pl.num_programs(0)
    channels, unused, columns = held.shape
    blocks = columns // BW
    group = grid_ref.shape[1] // BH

    @pl.when(step == 0)
    def first():
        acc[...] = jnp.zeros_like(acc)
        held[...] = top_ref[...]

    @pl.when(step == steps - 1)
    def last():
        held[...] = bottom_ref[...]

    @pl.when((step > 0) & (step < steps - 1))
    def inner():
        held[...] = cot_ref[...]

    for block in range(blocks):
        place = (step * blocks + block) * 4
        weight = (step * blocks + block) * 16
        row_off, row_st, col_off, col_st = [ints[place + k] for k in range(4)]
        rx = column_matrix(col_st, [floats[weight + 8 + k] for k in range(4)])
        ry = taps(grid_ref[...] - row_st, [floats[weight + k] for k in range(4)])
        piece = held[:, :, block * BW : (block + 1) * BW].reshape(channels * BH, BW)
        z = jnp.dot(piece, rx, preferred_element_type=jnp.float32).astype(jnp.bfloat16)
        rows = pl.ds(pl.multiple_of(row_off * 8, 8), 3 * BH // 2)
        cols = pl.ds(pl.multiple_of((col_off + 2 * block) * LANES, LANES), BW + LANES)
        for part in range(channels // group):
            spread = jnp.dot(
                ry,
                z[part * group * BH : (part + 1) * group * BH],
                preferred_element_type=jnp.float32,
            ).reshape(group, 3 * BH // 2, BW + LANES)
            where = (slice(part * group, (part + 1) * group), rows, cols)
            acc[where] = acc[where] + spread

    def finished():
        left = acc[:, :BH, BW : 2 * BW] + acc[:, :BH, columns + BW :]
        right = acc[:, :BH, columns : columns + BW] + acc[:, :BH, :BW]
        middle = acc[:, :BH, 2 * BW : columns]
        whole = jnp.concatenate([left, middle, right], axis=2)
        return jnp.swapaxes(whole, 0, 1).astype(jnp.bfloat16)[None]

    @pl.when((step >= 2) & (step % 2 == 0))
    def even():
        even_ref[...] = finished()

    @pl.when((step >= 2) & (step % 2 == 1))
    def odd():
        odd_ref[...] = finished()

    acc[:, :BH] = acc[:, BH : 2 * BH]
    acc[:, BH : 2 * BH] = acc[:, 2 * BH :]
    acc[:, 2 * BH :] = jnp.zeros((channels, BH, acc.shape[2]), jnp.float32)


def spread_call(ints, floats, cotangent, top, bottom):
    channels, band_rows, columns = cotangent.shape
    part = channels
    row_blocks = band_rows // BH
    group = 8
    across = np.arange(group * 3 * BH // 2)[:, None]
    along = np.arange(group * BH)[None, :]
    same = across // (3 * BH // 2) == along // BH
    grid = np.where(same, across % (3 * BH // 2) - along % BH, -1000).astype(np.int32)
    halo = pl.BlockSpec((part, BH, columns), lambda i, *s: (0, 0, 0))
    result = jax.ShapeDtypeStruct((row_blocks // 2, BH, part, columns), jnp.bfloat16)
    out_spec = pl.BlockSpec(
        (1, BH, part, columns), lambda i, *s: (jnp.maximum(i - 2, 0) // 2, 0, 0, 0)
    )
    flops = 2 * (row_blocks + 2) * (columns // BW) * part * BH * (BW + LANES) * (BW + 8 * 24)
    return pl.pallas_call(
        spread_kernel,
        grid_spec=pltpu.PrefetchScalarGridSpec(
            num_scalar_prefetch=2,
            grid=(row_blocks + 2,),
            in_specs=[
                pl.BlockSpec(
                    (part, BH, columns),
                    lambda i, *s: (0, jnp.clip(i - 1, 0, row_blocks - 1), 0),
                ),
                halo,
                halo,
                pl.BlockSpec(grid.shape, lambda i, *s: (0, 0)),
            ],
            out_specs=[out_spec, out_spec],
            scratch_shapes=[
                pltpu.VMEM((part, 3 * BH, columns + 2 * BW), jnp.float32),
                pltpu.VMEM((part, BH, columns), jnp.bfloat16),
            ],
        ),
        out_shape=[result, result],
        compiler_params=pltpu.CompilerParams(vmem_limit_bytes=VMEM_BYTES),
        cost_estimate=pl.CostEstimate(
            flops=flops, bytes_accessed=4 * part * band_rows * columns, transcendentals=0
        ),
        name="spread",
    )(ints, floats, cotangent, top, bottom, jnp.asarray(grid))


def frac_kernel(
    ints, floats, cot_ref, before_ref, here_ref, after_ref, top_ref, bottom_ref, grid_ref,
    out_ref, window, rx_both, ry_both
):
    step = pl.program_id(0)
    steps = pl.num_programs(0)
    channels, unused, columns = cot_ref.shape
    blocks = columns // BW
    group = grid_ref.shape[0] // BH

    def fill(rows, ref):
        window[:, rows, BW : columns + BW] = ref[...]
        window[:, rows, :BW] = ref[:, :, columns - BW :]
        window[:, rows, columns + BW :] = ref[:, :, :BW]

    @pl.when(step == 0)
    def first():
        fill(slice(0, BH), top_ref)

    @pl.when(step > 0)
    def before():
        fill(slice(0, BH), before_ref)

    fill(slice(BH, 2 * BH), here_ref)

    @pl.when(step == steps - 1)
    def last():
        fill(slice(2 * BH, 3 * BH), bottom_ref)

    @pl.when(step < steps - 1)
    def after():
        fill(slice(2 * BH, 3 * BH), after_ref)

    @pl.when(pl.program_id(1) == 0)
    def matrices():
        out_ref[...] = jnp.zeros_like(out_ref)
        for block in range(blocks):
            place = ((step + 1) * blocks + block) * 4
            weight = ((step + 1) * blocks + block) * 16
            row_off, row_st, unused_off, col_st = [ints[place + k] for k in range(4)]
            row_grid = grid_ref[...] - (row_off * 8 + row_st)
            ry_both[block, : group * BH] = taps(row_grid, [floats[weight + k] for k in range(4)])
            ry_both[block, group * BH :] = taps(
                row_grid, [floats[weight + 4 + k] for k in range(4)]
            )
            rx_both[block, :, : BW + LANES] = column_matrix(
                col_st, [floats[weight + 8 + k] for k in range(4)]
            )
            rx_both[block, :, BW + LANES :] = column_matrix(
                col_st, [floats[weight + 12 + k] for k in range(4)]
            )

    for block in range(blocks):
        col_off = ints[((step + 1) * blocks + block) * 4 + 2]
        cols = pl.ds(pl.multiple_of((col_off + 2 * block) * LANES, LANES), BW + LANES)
        piece = cot_ref[:, :, block * BW : (block + 1) * BW].reshape(channels * BH, BW)
        z = jnp.dot(piece, rx_both[block], preferred_element_type=jnp.float32)
        row_total = jnp.zeros((1, BW + LANES), jnp.float32)
        col_total = jnp.zeros((1, BW + LANES), jnp.float32)
        for part in range(channels // group):
            source = window[part * group : (part + 1) * group, :, cols]
            source = source.reshape(group * 3 * BH, BW + LANES)
            lifted = jnp.dot(ry_both[block], source, preferred_element_type=jnp.float32)
            zs = z[part * group * BH : (part + 1) * group * BH]
            row_total += jnp.sum(
                lifted[group * BH :] * zs[:, : BW + LANES], axis=0, keepdims=True
            )
            col_total += jnp.sum(
                lifted[: group * BH] * zs[:, BW + LANES :], axis=0, keepdims=True
            )
        out_ref[0, block : block + 1] += row_total
        out_ref[0, blocks + block : blocks + block + 1] += col_total


def frac_call(ints, floats, cotangent, advected, top, bottom):
    channels, band_rows, columns = cotangent.shape
    part = 16
    row_blocks = band_rows // BH
    blocks = columns // BW
    group = 8
    across = np.arange(group * BH)[:, None]
    along = np.arange(group * 3 * BH)[None, :]
    same = across // BH == along // (3 * BH)
    grid = np.where(same, along % (3 * BH) - across % BH, -1000).astype(np.int32)

    def rows(shift):
        return pl.BlockSpec(
            (part, BH, columns),
            lambda i, c, *s: (c, jnp.clip(i + shift, 0, row_blocks - 1), 0),
        )

    halo = pl.BlockSpec((part, BH, columns), lambda i, c, *s: (c, 0, 0))
    flops = 2 * row_blocks * blocks * channels * BH * (BW + LANES) * (2 * BW + 2 * group * 3 * BH)
    return pl.pallas_call(
        frac_kernel,
        grid_spec=pltpu.PrefetchScalarGridSpec(
            num_scalar_prefetch=2,
            grid=(row_blocks, channels // part),
            in_specs=[
                rows(0),
                rows(-1),
                rows(0),
                rows(1),
                halo,
                halo,
                pl.BlockSpec(grid.shape, lambda i, c, *s: (0, 0)),
            ],
            out_specs=pl.BlockSpec((1, 2 * blocks, BW + LANES), lambda i, c, *s: (i, 0, 0)),
            scratch_shapes=[
                pltpu.VMEM((part, 3 * BH, columns + 2 * BW), jnp.bfloat16),
                pltpu.VMEM((blocks, BW, 2 * (BW + LANES)), jnp.bfloat16),
                pltpu.VMEM((blocks, 2 * group * BH, group * 3 * BH), jnp.bfloat16),
            ],
        ),
        out_shape=jax.ShapeDtypeStruct((row_blocks, 2 * blocks, BW + LANES), jnp.float32),
        compiler_params=pltpu.CompilerParams(vmem_limit_bytes=VMEM_BYTES),
        cost_estimate=pl.CostEstimate(
            flops=flops, bytes_accessed=8 * channels * band_rows * columns, transcendentals=0
        ),
        name="frac",
    )(ints, floats, cotangent, advected, advected, advected, top, bottom, jnp.asarray(grid))


def mlp_kernel(*refs):
    x_ref, dy_ref, w_in_ref, w_in_t_ref, bias_ref, w_out_ref = refs[:6]
    dx_ref, first_ref, shift_ref, second_ref, x_flat, dy_flat, dx_rows = refs[-7:]
    width = x_ref.shape[2]

    @pl.when(pl.program_id(0) == 0)
    def clear():
        first_ref[...] = jnp.zeros_like(first_ref)
        shift_ref[...] = jnp.zeros_like(shift_ref)
        second_ref[...] = jnp.zeros_like(second_ref)

    x_rows = jnp.swapaxes(x_ref[...].astype(jnp.float32), 0, 1).astype(jnp.bfloat16)
    for row in range(BH):
        cols = slice(row * width, (row + 1) * width)
        x_flat[:, cols] = x_rows[row]
        dy_flat[:, :, cols] = dy_ref[:, row]
    tile = 1024
    for start in range(0, BH * width, tile):
        cols = slice(start, start + tile)
        x = x_flat[:, cols]
        dy = dy_flat[:, :, cols].reshape(x.shape)
        pre = jnp.dot(w_in_t_ref[...], x, preferred_element_type=jnp.float32) + bias_ref[...]
        sigma = jax.nn.sigmoid(pre)
        act = (pre * sigma).astype(jnp.bfloat16)
        dact = jnp.dot(w_out_ref[...], dy, preferred_element_type=jnp.float32)
        dpre_wide = dact * sigma * (1.0 + pre * (1.0 - sigma))
        dpre = dpre_wide.astype(jnp.bfloat16)
        dx = dy.astype(jnp.float32) + jnp.dot(
            w_in_ref[...], dpre, preferred_element_type=jnp.float32
        )
        for part in range(tile // width):
            dx_rows[start // width + part] = dx[:, part * width : (part + 1) * width]
        first_ref[...] += contract_points(x, dpre)
        second_ref[...] += contract_points(act, dy)
        shift_ref[...] += jnp.sum(dpre.astype(jnp.float32), axis=1, keepdims=True)
    dx_ref[...] = jnp.swapaxes(dx_rows[...], 0, 1).astype(jnp.bfloat16)


def mlp_call(inputs, dy, w_in, bias_in, w_out, half, earlier):
    channels, point_rows, columns = inputs.shape
    hidden = w_in.shape[1]
    sources, unused, part, unused_columns = dy.shape
    width = LANES
    whole = lambda shape: pl.BlockSpec(shape, lambda j: (0, 0))
    points = pl.BlockSpec((channels, BH, width), lambda j: (0, half, j))
    dy_spec = pl.BlockSpec((sources, BH, part, width), lambda j: (0, 0, 0, j))
    operands = [inputs, dy, w_in, w_in.T, bias_in[:, None], w_out]
    in_specs = [
        points,
        dy_spec,
        whole((channels, hidden)),
        whole((hidden, channels)),
        whole((hidden, 1)),
        whole((hidden, channels)),
    ]
    aliases = {}
    if earlier is not None:
        operands.append(earlier)
        in_specs.append(pl.BlockSpec(memory_space=pl.ANY))
        aliases = {6: 0}
    return pl.pallas_call(
        mlp_kernel,
        grid=(columns // width,),
        in_specs=in_specs,
        out_specs=[
            points,
            whole((channels, hidden)),
            whole((hidden, 1)),
            whole((hidden, channels)),
        ],
        out_shape=[
            jax.ShapeDtypeStruct(inputs.shape, jnp.bfloat16),
            jax.ShapeDtypeStruct((channels, hidden), jnp.float32),
            jax.ShapeDtypeStruct((hidden, 1), jnp.float32),
            jax.ShapeDtypeStruct((hidden, channels), jnp.float32),
        ],
        scratch_shapes=[
            pltpu.VMEM((channels, BH * width), jnp.bfloat16),
            pltpu.VMEM((sources, part, BH * width), jnp.bfloat16),
            pltpu.VMEM((BH, channels, width), jnp.float32),
        ],
        input_output_aliases=aliases,
        compiler_params=pltpu.CompilerParams(vmem_limit_bytes=VMEM_BYTES),
        cost_estimate=pl.CostEstimate(
            flops=10 * channels * hidden * BH * columns,
            bytes_accessed=6 * channels * BH * columns,
            transcendentals=2 * hidden * BH * columns,
        ),
        name="mlp",
    )(*operands)


def scattered(parts, axis):
    return jnp.sum(lax.all_to_all(parts, axis, split_axis=0, concat_axis=0, tiled=True), axis=0)


def parts_of(grid, axis):
    count = lax.axis_size(axis)
    return grid.reshape((count, grid.shape[0] // count) + grid.shape[1:])


def neighbours(cells, axis, dim, width):
    count = lax.axis_size(axis)
    ends = count - 1
    head = lax.slice_in_dim(cells, 0, width, axis=dim)
    tail = lax.slice_in_dim(cells, cells.shape[dim] - width, cells.shape[dim], axis=dim)
    return (
        lax.ppermute(tail, axis, [(i, i + 1) for i in range(ends)]),
        lax.ppermute(head, axis, [(i + 1, i) for i in range(ends)]),
    )


def fast_shards(
    inputs, w_in, bias_in, w_out, advected, cotangent, offsets, stencil_row, stencil_col, fracs
):
    band_rows, columns = advected.shape[1:]
    hidden = w_in.shape[1]
    blocks = columns // BW
    row_blocks = band_rows // BH
    places = jnp.stack([offsets[0], stencil_row, offsets[1], stencil_col], axis=-1)
    table = jnp.concatenate([places.astype(jnp.float32), jnp.moveaxis(fracs, 0, -1)], axis=-1)
    above, below = neighbours(table, "lat", 0, 1)
    table = jnp.concatenate([above, table, below], axis=0)
    ints = table[..., :4].astype(jnp.int32).reshape(-1)
    row_w, row_s = catmull(table[..., 4])
    col_w, col_s = catmull(table[..., 5])
    floats = jnp.stack([*row_w, *row_s, *col_w, *col_s], axis=-1).reshape(-1)

    cot_top, cot_bottom = neighbours(cotangent, "lat", 1, BH)

    def to_points(cells):
        return lax.all_to_all(cells, "grp", split_axis=0, concat_axis=0, tiled=True)

    even, odd = spread_call(ints, floats, cotangent, cot_top, cot_bottom)
    dy_even = to_points(even)
    adv_top, adv_bottom = neighbours(advected, "lat", 1, BH)
    frac_parts = frac_call(ints, floats, cotangent, advected, adv_top, adv_bottom)
    odd, dy_even, frac_parts = lax.optimization_barrier((odd, dy_even, frac_parts))
    dy_odd = to_points(odd)
    frac_local = jnp.sum(frac_parts, axis=2).reshape(row_blocks, 2, blocks)
    frac_local = jnp.moveaxis(frac_local, 1, 0)

    early = mlp_call(inputs, dy_even, w_in, bias_in, w_out, 0, None)
    late = mlp_call(inputs, dy_odd, w_in, bias_in, w_out, 1, early[0])
    first, shift, second = [early[k] + late[k] for k in (1, 2, 3)]
    merged = jnp.concatenate([first.T, second, jnp.broadcast_to(shift, (hidden, LANES))], axis=1)
    parts = parts_of(scattered(parts_of(merged, "lat"), "lat"), "grp")
    count, depth, width = parts.shape
    extra = -(-frac_local.size // width)
    padded = jnp.pad(frac_local.reshape(-1), (0, extra * width - frac_local.size))
    every = jnp.broadcast_to(padded.reshape(1, extra, width), (count, extra, width))
    share = scattered(jnp.concatenate([parts, every], axis=1), "grp")
    frac_total = share[depth:].reshape(-1)[: frac_local.size].reshape(frac_local.shape)
    grad_frac = frac_total / math.sqrt(C * BH * BW)
    total_points = band_rows * columns * lax.axis_size("lat")
    share = share[:depth] * (1.0 / math.sqrt(total_points))
    return (late[0], share[:, :C].T, share[:, 2 * C], share[:, C : 2 * C], grad_frac)


def solution(mesh):
    grp = mesh.shape["grp"]

    def chosen(*args):
        band_rows = args[4].shape[1]
        channels = args[4].shape[0]
        paired = args[0].shape[1] == 2 * BH and band_rows == 2 * BH * grp
        return (fast_shards if paired and channels % 32 == 0 else shards)(*args)

    placed = (
        P(None, ("lat", "grp"), None),
        P(),
        P(),
        P(),
        P("grp", "lat", None),
        P("grp", "lat", None),
        P(None, "lat", None),
        P("lat", None),
        P("lat", None),
        P(None, "lat", None),
    )
    return jax.shard_map(
        chosen,
        mesh=mesh,
        in_specs=placed,
        out_specs=(
            P(None, ("lat", "grp"), None),
            P(None, ("lat", "grp")),
            P(("lat", "grp")),
            P(("lat", "grp"), None),
            P(None, "lat", None),
        ),
        check_vma=False,
    )
```
